1024 devices in a mesh: dp: 16 (over y, core), expert: 64 (over z, x).
Axes of the slice: x: 4, y: 8, z: 16, core: 2. Of those that a mesh axis runs over, the one named last changes fastest.
Arguments:
- out_grad: bfloat16 [16384, 4096], P(('dp', 'expert')), may hold values from -6 to 6
- hidden: bfloat16 [16384, 8, 768], P(('dp', 'expert')), may hold values from -3 to 3
- combine: float32 [16384, 8], P(('dp', 'expert')), may hold values from 0.02 to 0.5
- expert_ids: int32 [16384, 8], P(('dp', 'expert')), may hold values from 0 to 63, all different within a row; in each aligned block of 16 rows (0 to 15, 16 to 31, ...) at most 3 rows name the same one
- down_weight: bfloat16 [64, 4096, 768], P('expert'), may hold values from -0.21875 to 0.21875
Outputs:
- grad_hidden: bfloat16 [16384, 8, 768], P(('dp', 'expert'))
- grad_weights: float32 [16384, 8], P(('dp', 'expert'))
- grad_down: bfloat16 [64, 4096, 768], P('expert', 'dp')
The draws below stay inside these ranges and needn't reach their ends.
Inputs may be any that keep to these rules, and one draw needn't show every extreme that they name: `expert_ids`: among the 16 tokens of one device no expert is named more than 3 times, a bound that some block reaches; the 8 experts of a token are different.
All inputs are finite; a program needn't handle non-finite values.
Results may differ from the reference program's by a relative error of at most 0.022.
Values may be sent and summed in bfloat16 or wider, within the bound.
No kernel may reach another device: no remote copies, remote signals or barrier semaphores. Data moves between devices by JAX's collectives and lax.ppermute only.
A program may use at most 64 MiB of HBM per device.

```python
import math
import jax
import jax.numpy as jnp
import numpy as np
from jax import lax

D = 4096
FF = 768
TOPK = 8
TOK_DEV = 16
EXPERTS = 64
CAP = 3
TOKENS = 16384
N_DP = 16
N_EXPERT = 64


def block_scale(key, dims, shards, smallest, largest):
    loudness = 1.0
    for axis_at, shards_of in shards:
        steps = jax.random.uniform(jax.random.fold_in(jax.random.fold_in(key, 6), axis_at), (shards_of,), jnp.float32, smallest / len(shards), largest / len(shards))
        loudness = loudness * jnp.repeat(jnp.exp(steps), dims[axis_at] // shards_of).reshape((-1,) + (1,) * (len(dims) - 1 - axis_at))
    return loudness


def deal_out(rng, own, number, rows, amount, top, limit, skew):
    ranking = jax.random.permutation(rng, amount)
    packed, usual = load_shares(amount, rows * top, limit, skew, True), load_shares(amount, rows * top, limit, skew, False)
    places = jnp.arange(amount)

    def named(sizes, offset_by):
        used = int((sizes > 0).sum())
        fixed = max(1, used // 4)
        moved = fixed + (places - fixed + offset_by * (used - fixed)) % max(1, amount - fixed)
        return jnp.zeros((amount,), jnp.int32).at[ranking[jnp.where(places < fixed, places, moved)]].set(jnp.asarray(sizes, jnp.int32))

    sizes = jnp.where(number % 4 == 0, named(packed, number // 4), named(usual, number - number // 4 - 1))
    mixed = jax.random.permutation(jax.random.fold_in(own, 3), amount)
    source_of, sink = mixed[0:amount // 2 * 2:2], mixed[1:amount // 2 * 2:2]
    slack = jnp.minimum(sizes[source_of] - 1, limit - sizes[sink]) // 2
    slack = jnp.where((source_of == ranking[0]) | (sink == ranking[0]) | (sizes[sink] == 0), 0, jnp.maximum(slack, 0))
    moved = jax.random.randint(jax.random.fold_in(own, 4), (amount // 2,), 0, 1 << 20) % (slack + 1)
    sizes = sizes.at[source_of].add(-moved).at[sink].add(moved)
    labels = jnp.searchsorted(jnp.cumsum(sizes), jnp.arange(rows * top), side="right").astype(jnp.int32)
    listing = labels.reshape(top, rows).T
    listing = listing[jax.random.permutation(jax.random.fold_in(own, 1), rows)]
    offset_by = jax.random.randint(jax.random.fold_in(own, 2), (rows, 1), 0, top)
    return jnp.take_along_axis(listing, (jnp.arange(top)[None, :] + offset_by) % top, axis=1)


def load_shares(amount, total, limit, lean, full):
    loads = [(1 << 20) // math.isqrt(standing ** lean) + 1 for standing in range(1, amount + 1)]
    largest = limit if full else min(limit, max(-(-total // amount), total * loads[0] // sum(loads)))
    least = 1 if total - largest >= amount - 1 else 0
    counts, rest = [largest] + [least] * (amount - 1), total - largest - least * (amount - 1)
    while rest > 0:
        free = [i for i in range(1, amount) if counts[i] < largest] or [i for i in range(1, amount) if counts[i] < limit]
        pool, left = sum([loads[i] for i in free]), rest
        for i in free:
            more = min(limit - counts[i], max(1, left * loads[i] // pool), rest)
            counts[i] = counts[i] + more
            rest = rest - more
    return np.array(counts)


def gaussian(stream_key, dims, spread, bound, pieces=(), kind=jnp.bfloat16):
    values = spread * jax.random.normal(stream_key, dims, jnp.float32)
    if pieces:
        values = values * block_scale(stream_key, dims, pieces, -0.22, 0.18)
    return jnp.clip(values, -bound, bound).astype(kind)


def setup_inputs(seed: int = 0) -> dict:
    key_list = jax.random.split(jax.random.key(seed), 6)
    out_grad = gaussian(key_list[0], (TOKENS, D), 0.5, 6.0, ((0, 1024),))
    hidden = gaussian(key_list[1], (TOKENS, TOPK, FF), 0.2, 3.0, ((0, 1024),))
    combine = jnp.clip(jnp.exp(math.log(0.5) - 3.218876 * jax.random.uniform(key_list[2], (TOKENS, TOPK), jnp.float32) ** block_scale(key_list[2], (TOKENS, TOPK), ((0, 1024),), -0.2, 0.2)), 0.02, 0.5)
    expert_ids_keys = jax.random.split(jax.random.fold_in(key_list[3], 1), TOKENS // TOK_DEV)
    expert_ids_turns = jax.random.permutation(jax.random.fold_in(key_list[3], 3), TOKENS // TOK_DEV)
    expert_ids = jax.vmap(lambda own, number: deal_out(jax.random.fold_in(key_list[3], 2), own, number, TOK_DEV, EXPERTS, TOPK, CAP, 2))(expert_ids_keys, expert_ids_turns).reshape((TOKENS, TOPK))
    down_weight = gaussian(key_list[4], (EXPERTS, D, FF), FF ** -0.5, 0.21875, ((0, 64),))
    return dict(out_grad=out_grad, hidden=hidden, combine=combine, expert_ids=expert_ids, down_weight=down_weight)


def reference(out_grad, hidden, combine, expert_ids, down_weight):
    blocks = N_DP * N_EXPERT
    rows = TOK_DEV * TOPK
    slots_all = blocks * CAP
    ids_block = expert_ids.reshape(blocks, rows)
    onehot = (ids_block[:, :, None] == jnp.arange(EXPERTS, dtype=jnp.int32)[None, None, :]).astype(jnp.int32)
    before = jnp.cumsum(onehot, axis=1) - onehot
    slot = jnp.sum(onehot * before, axis=2).astype(jnp.int32)
    block_of = jnp.arange(blocks, dtype=jnp.int32)[:, None]
    position = (block_of * CAP + slot).reshape(TOKENS * TOPK).astype(jnp.int32)
    flat_ids = expert_ids.reshape(TOKENS * TOPK)
    target = (flat_ids * slots_all + position).astype(jnp.int32)
    pair_index = jnp.arange(TOKENS * TOPK, dtype=jnp.int32)
    token_table = jnp.full((EXPERTS * slots_all,), TOKENS, jnp.int32).at[target].set(pair_index // TOPK)
    pair_table = jnp.full((EXPERTS * slots_all,), TOKENS * TOPK, jnp.int32).at[target].set(pair_index)
    token_table = token_table.reshape(EXPERTS, slots_all)
    pair_table = pair_table.reshape(EXPERTS, slots_all)
    weighted = (combine[:, :, None] * hidden.astype(jnp.float32)).astype(jnp.bfloat16)
    grad_pad = jnp.concatenate([out_grad, jnp.zeros((1, D), jnp.bfloat16)], axis=0)
    weighted_pad = jnp.concatenate([weighted.reshape(TOKENS * TOPK, FF), jnp.zeros((1, FF), jnp.bfloat16)], axis=0)

    def one_expert(inputs):
        tokens_here, pairs_here, weight_here = inputs
        grads = grad_pad[tokens_here]
        acts = weighted_pad[pairs_here]
        projected = jnp.dot(grads, weight_here, preferred_element_type=jnp.float32).astype(jnp.bfloat16)
        grouped_grads = grads.astype(jnp.float32).reshape(N_DP, N_EXPERT * CAP, D)
        grouped_acts = acts.astype(jnp.float32).reshape(N_DP, N_EXPERT * CAP, FF)
        partial_value = jnp.einsum('gmd,gmf->gdf', grouped_grads, grouped_acts).astype(jnp.bfloat16)
        partial_value = lax.optimization_barrier(partial_value)
        summed = jnp.sum(partial_value.astype(jnp.float32), axis=0).astype(jnp.bfloat16)
        return projected, summed

    projected_all, grad_down = lax.map(one_expert, (token_table, pair_table, down_weight))
    back = projected_all.reshape(EXPERTS * slots_all, FF)[target].reshape(TOKENS, TOPK, FF).astype(jnp.float32)
    grad_hidden = (combine[:, :, None] * back).astype(jnp.bfloat16)
    grad_weights = jnp.sum(hidden.astype(jnp.float32) * back, axis=2)
    return grad_hidden, grad_weights, grad_down
```

```python
import jax
import jax.numpy as jnp
from jax import lax
from jax.sharding import Mesh
from jax.sharding import PartitionSpec as P

CORES = 2
XS = 4
DIRECT = 1280
F32 = jnp.float32
BF16 = jnp.bfloat16


def dot(a, b, dims=(((1,), (0,)), ((), ()))):
    return lax.dot_general(a, b, dims, preferred_element_type=F32)


def local(out_grad, hidden, combine, expert_ids, down_weight):
    tok, width = out_grad.shape
    topk = expert_ids.shape[1]
    ffw = hidden.shape[2]
    xs, zs, ys = lax.axis_size("x"), lax.axis_size("z"), lax.axis_size("y")
    core, z_here = lax.axis_index("core"), lax.axis_index("z")
    owners = xs * zs
    cap = min(tok, 3 * tok * topk // (2 * owners))
    rows = tok * topk
    slots_here = owners * cap
    half = width // CORES
    direct = DIRECT // CORES
    relay = half - direct
    piece = half // ys

    by_core = (
        out_grad.reshape(tok, ys, CORES, piece).transpose(0, 2, 1, 3).reshape(tok, CORES, half)
    )
    ids_wide = jnp.pad(expert_ids.astype(BF16), ((0, 0), (0, 128 - topk)))
    relay_send = jnp.concatenate(
        [by_core[:, 0, direct:], by_core[:, 1, direct:], ids_wide], axis=1
    )
    relay_all = lax.all_gather(relay_send, "z", axis=0, tiled=True)

    flat_ids = expert_ids.reshape(rows)
    owner = (flat_ids % xs) * zs + flat_ids // xs
    onehot = (owner[:, None] == jnp.arange(owners, dtype=jnp.int32)[None, :]).astype(jnp.int32)
    before = jnp.cumsum(onehot, axis=0) - onehot
    slot = jnp.sum(onehot * before, axis=1)
    target = owner * cap + slot
    placing = (target[None, :] == jnp.arange(slots_here, dtype=jnp.int32)[:, None]).astype(BF16)
    by_token = jnp.sum(placing.reshape(slots_here, tok, topk).astype(F32), axis=2).astype(BF16)
    weighted = (combine[:, :, None] * hidden.astype(F32)).astype(BF16).reshape(rows, ffw)
    direct_cols = jnp.concatenate([by_core[:, 0, :direct], by_core[:, 1, :direct]], axis=1)
    send = jnp.concatenate(
        [dot(placing, weighted).astype(BF16), dot(by_token, direct_cols).astype(BF16)], axis=1
    )
    wide = send.shape[1]
    got = lax.all_to_all(
        send.reshape(owners, cap * wide // 128, 128),
        ("x", "z"),
        split_axis=0,
        concat_axis=0,
        tiled=True,
    ).reshape(slots_here, wide)
    acts = got[:, :ffw]
    got_direct = got[:, ffw:]

    seen = relay_all[:, CORES * relay : CORES * relay + topk].astype(jnp.int32)
    experts_here = z_here * xs + jnp.arange(xs, dtype=jnp.int32)
    names = jnp.any(seen[:, :, None] == experts_here[None, None, :], axis=1)
    names = names.reshape(zs, tok, xs).astype(jnp.int32)
    nth = jnp.cumsum(names, axis=1) - names
    chosen = (names[None] > 0) & (nth[None] == jnp.arange(cap, dtype=jnp.int32)[:, None, None, None])
    chosen = chosen.transpose(3, 1, 0, 2)
    picking = (
        chosen[:, :, :, None, :]
        & (jnp.arange(zs)[:, None] == jnp.arange(zs)[None, :])[None, :, None, :, None]
    )
    picking = picking.astype(BF16).reshape(slots_here, zs * tok)
    relay_rows = dot(picking, relay_all[:, : CORES * relay]).astype(BF16)
    got_relay = lax.all_to_all(
        relay_rows.reshape(xs, zs * cap, CORES * relay), "x", split_axis=0, concat_axis=0, tiled=True
    ).reshape(slots_here, CORES * relay)

    halves = [
        jnp.concatenate(
            [
                got_direct[:, c * direct : (c + 1) * direct],
                got_relay[:, c * relay : (c + 1) * relay],
            ],
            axis=1,
        )
        for c in range(CORES)
    ]
    mine = jnp.where(core == 0, halves[0], halves[1])
    theirs = jnp.where(core == 0, halves[1], halves[0])
    swap = [(0, 1), (1, 0)]
    other_acts = lax.ppermute(acts, "core", swap)
    other_grad = lax.ppermute(theirs, "core", swap)

    rows_dim = (((0,), (0,)), ((), ()))
    partial_value = dot(
        jnp.concatenate([mine, other_grad], axis=0),
        jnp.concatenate([acts, other_acts], axis=0),
        rows_dim,
    ).astype(BF16)
    grad_down = lax.psum_scatter(partial_value, "y", scatter_dimension=0, tiled=True)

    weight = down_weight[0].reshape(ys, CORES, piece, ffw)
    projected = sum(
        dot(halves[c], weight[:, c].reshape(half, ffw)) for c in range(CORES)
    ).astype(BF16)
    returned = lax.all_to_all(
        projected.reshape(owners, cap * ffw // 1152, 1152),
        ("x", "z"),
        split_axis=0,
        concat_axis=0,
        tiled=True,
    ).reshape(slots_here, ffw)
    back = dot(placing, returned, rows_dim).reshape(tok, topk, ffw)
    grad_hidden = (combine[:, :, None] * back).astype(BF16)
    grad_weights = jnp.sum(hidden.astype(F32) * back, axis=2)
    return (grad_hidden, grad_weights, grad_down[None])


def solution(mesh):
    dp, expert = mesh.shape["dp"], mesh.shape["expert"]
    fine = Mesh(
        mesh.devices.reshape(dp // CORES, CORES, expert // XS, XS), ("y", "core", "z", "x")
    )
    tokens = ("y", "core", "z", "x")
    placed = (
        P(tokens, None),
        P(tokens, None, None),
        P(tokens, None),
        P(tokens, None),
        P(("z", "x"), None, None),
    )
    return jax.shard_map(
        local,
        mesh=fine,
        in_specs=placed,
        out_specs=(
            P(tokens, None, None),
            P(tokens, None),
            P(("z", "x"), ("y", "core"), None),
        ),
        check_vma=False,
    )
```

```python
import jax
import jax.numpy as jnp
from jax import lax
from jax.sharding import Mesh
from jax.sharding import PartitionSpec as P

CORES = 2
XS = 4
FIRST = 896
F32 = jnp.float32
BF16 = jnp.bfloat16


def dot(a, b, dims=(((1,), (0,)), ((), ()))):
    return lax.dot_general(a, b, dims, preferred_element_type=F32)


def local(out_grad, hidden, combine, expert_ids, down_weight):
    tok, width = out_grad.shape
    topk = expert_ids.shape[1]
    ffw = hidden.shape[2]
    xs, zs, ys = lax.axis_size("x"), lax.axis_size("z"), lax.axis_size("y")
    core, z_here = lax.axis_index("core"), lax.axis_index("z")
    owners = xs * zs
    cap = min(tok, 3 * tok * topk // (2 * owners))
    rows = tok * topk
    slots_here = owners * cap
    half = width // CORES
    piece = half // ys
    first = FIRST
    second = half - first

    by_core = (
        out_grad.reshape(tok, ys, CORES, piece).transpose(0, 2, 1, 3).reshape(tok, CORES, half)
    )
    all_second = lax.all_gather(
        by_core[:, :, first:].reshape(tok, CORES * second), "z", axis=0, tiled=True
    )
    ids_wide = jnp.pad(expert_ids.astype(BF16), ((0, 0), (0, 128 - topk)))
    all_first = lax.all_gather(
        jnp.concatenate([ids_wide, by_core[:, 0, :first], by_core[:, 1, :first]], axis=1),
        "z",
        axis=0,
        tiled=True,
    )

    flat_ids = expert_ids.reshape(rows)
    owner = (flat_ids % xs) * zs + flat_ids // xs
    onehot = (owner[:, None] == jnp.arange(owners, dtype=jnp.int32)[None, :]).astype(jnp.int32)
    before = jnp.cumsum(onehot, axis=0) - onehot
    slot = jnp.sum(onehot * before, axis=1)
    target = owner * cap + slot
    placing = (target[None, :] == jnp.arange(slots_here, dtype=jnp.int32)[:, None]).astype(BF16)
    weighted = (combine[:, :, None] * hidden.astype(F32)).astype(BF16).reshape(rows, ffw)
    acts = lax.all_to_all(
        dot(placing, weighted).astype(BF16).reshape(owners, 2, cap * ffw // 2),
        ("x", "z"),
        split_axis=0,
        concat_axis=0,
        tiled=True,
    ).reshape(slots_here, ffw)

    seen = all_first[:, :topk].astype(jnp.int32)
    experts_here = z_here * xs + jnp.arange(xs, dtype=jnp.int32)
    names = jnp.any(seen[:, :, None] == experts_here[None, None, :], axis=1)
    names = names.reshape(zs, tok, xs).astype(jnp.int32)
    nth = jnp.cumsum(names, axis=1) - names
    chosen = (names[None] > 0) & (nth[None] == jnp.arange(cap, dtype=jnp.int32)[:, None, None, None])
    chosen = chosen.transpose(3, 1, 0, 2)
    picking = (
        chosen[:, :, :, None, :]
        & (jnp.arange(zs)[:, None] == jnp.arange(zs)[None, :])[None, :, None, :, None]
    )
    picking = picking.astype(BF16).reshape(slots_here, zs * tok)
    picking, acts = lax.optimization_barrier((picking, acts))

    def relay(gathered):
        return lax.all_to_all(
            dot(picking, gathered).astype(BF16).reshape(xs, zs * cap, gathered.shape[1]),
            "x",
            split_axis=0,
            concat_axis=0,
            tiled=True,
        ).reshape(slots_here, gathered.shape[1])

    got_first = relay(all_first[:, 128:])
    got_second = relay(all_second)
    halves = [
        jnp.concatenate(
            [
                got_first[:, c * first : (c + 1) * first],
                got_second[:, c * second : (c + 1) * second],
            ],
            axis=1,
        )
        for c in range(CORES)
    ]
    mine = jnp.where(core == 0, halves[0], halves[1])
    theirs = jnp.where(core == 0, halves[1], halves[0])
    swap = [(0, 1), (1, 0)]
    other_acts = lax.ppermute(acts, "core", swap)
    other_grad = lax.ppermute(theirs, "core", swap)

    rows_dim = (((0,), (0,)), ((), ()))
    partial_value = dot(
        jnp.concatenate([mine, other_grad], axis=0),
        jnp.concatenate([acts, other_acts], axis=0),
        rows_dim,
    ).astype(BF16)
    grad_down = lax.psum_scatter(partial_value, "y", scatter_dimension=0, tiled=True)

    weight = down_weight[0].reshape(ys, CORES, piece, ffw)
    projected = sum(
        dot(halves[c], weight[:, c].reshape(half, ffw)) for c in range(CORES)
    ).astype(BF16)
    returned = lax.all_to_all(
        projected.reshape(owners, cap * ffw // 1152, 1152),
        ("x", "z"),
        split_axis=0,
        concat_axis=0,
        tiled=True,
    ).reshape(slots_here, ffw)
    back = dot(placing, returned, rows_dim).reshape(tok, topk, ffw)
    grad_hidden = (combine[:, :, None] * back).astype(BF16)
    grad_weights = jnp.sum(hidden.astype(F32) * back, axis=2)
    return (grad_hidden, grad_weights, grad_down[None])


def solution(mesh):
    dp, expert = mesh.shape["dp"], mesh.shape["expert"]
    fine = Mesh(
        mesh.devices.reshape(dp // CORES, CORES, expert // XS, XS), ("y", "core", "z", "x")
    )
    tokens = ("y", "core", "z", "x")
    placed = (
        P(tokens, None),
        P(tokens, None, None),
        P(tokens, None),
        P(tokens, None),
        P(("z", "x"), None, None),
    )
    return jax.shard_map(
        local,
        mesh=fine,
        in_specs=placed,
        out_specs=(
            P(tokens, None, None),
            P(tokens, None),
            P(("z", "x"), ("y", "core"), None),
        ),
        check_vma=False,
    )
```

```python
import jax
import jax.numpy as jnp
from jax import lax
from jax.sharding import Mesh
from jax.sharding import PartitionSpec as P

CORES = 2
XS = 4
PAIR = 2
DIRECT = 128
F32 = jnp.float32
BF16 = jnp.bfloat16


def dot(a, b, dims=(((1,), (0,)), ((), ()))):
    return lax.dot_general(a, b, dims, preferred_element_type=F32)


def exchange(value, axes):
    return lax.all_to_all(value, axes, split_axis=0, concat_axis=0, tiled=True)


def local(out_grad, hidden, combine, expert_ids, down_weight):
    tok, width = out_grad.shape
    topk = expert_ids.shape[1]
    ffw = hidden.shape[2]
    xs, ys = lax.axis_size("x"), lax.axis_size("y")
    far, near = lax.axis_size("far"), lax.axis_size("near")
    core, far_here = lax.axis_index("core"), lax.axis_index("far")
    owners = far * near * xs
    plane = near * xs
    cap = min(tok, 3 * tok * topk // (2 * owners))
    rows = tok * topk
    slots_here = owners * cap
    half = width // CORES
    piece = half // ys
    relayed = half - DIRECT

    flat_ids = expert_ids.reshape(rows)
    owner = (flat_ids % plane) * far + flat_ids // plane
    onehot = (owner[:, None] == jnp.arange(owners, dtype=jnp.int32)[None, :]).astype(jnp.int32)
    before = jnp.cumsum(onehot, axis=0) - onehot
    slot = jnp.sum(onehot * before, axis=1)
    target = owner * cap + slot
    placing = (target[None, :] == jnp.arange(slots_here, dtype=jnp.int32)[:, None]).astype(BF16)
    by_token = jnp.sum(placing.reshape(slots_here, tok, topk).astype(F32), axis=2).astype(BF16)
    weighted = (combine[:, :, None] * hidden.astype(F32)).astype(BF16).reshape(rows, ffw)

    by_core = (
        out_grad.reshape(tok, ys, CORES, piece).transpose(0, 2, 1, 3).reshape(tok, CORES, half)
    )
    direct_cols = by_core[:, :, :DIRECT].reshape(tok, CORES * DIRECT)
    send = jnp.concatenate(
        [dot(placing, weighted).astype(BF16), dot(by_token, direct_cols).astype(BF16)], axis=1
    )
    wide = send.shape[1]
    got = exchange(
        send.reshape(owners, cap * wide // 128, 128), ("near", "x", "far")
    ).reshape(slots_here, wide)

    ids_wide = jnp.pad(expert_ids.astype(BF16), ((0, 0), (0, 128 - topk)))
    gathered = lax.all_gather(
        jnp.concatenate([ids_wide, by_core[:, 0, DIRECT:], by_core[:, 1, DIRECT:]], axis=1),
        "far",
        axis=0,
        tiled=True,
    )

    seen = gathered[:, :topk].astype(jnp.int32)
    experts_here = far_here * plane + jnp.arange(plane, dtype=jnp.int32)
    names = jnp.any(seen[:, :, None] == experts_here[None, None, :], axis=1)
    names = names.reshape(far, tok, plane).astype(jnp.int32)
    nth = jnp.cumsum(names, axis=1) - names
    chosen = (names[None] > 0) & (nth[None] == jnp.arange(cap, dtype=jnp.int32)[:, None, None, None])
    chosen = chosen.transpose(3, 1, 0, 2)
    picking = (
        chosen[:, :, :, None, :]
        & (jnp.arange(far)[:, None] == jnp.arange(far)[None, :])[None, :, None, :, None]
    )
    picking = picking.astype(BF16).reshape(slots_here, far * tok)
    picking, got = lax.optimization_barrier((picking, got))
    relay_rows = dot(picking, gathered[:, 128:]).astype(BF16)
    got_relay = exchange(
        relay_rows.reshape(plane, far * cap, CORES * relayed), ("near", "x")
    ).reshape(slots_here, CORES * relayed)

    swap = [(0, 1), (1, 0)]
    acts = got[:, :ffw]
    both_acts = jnp.concatenate([acts, lax.ppermute(acts, "core", swap)], axis=0)
    weight = down_weight[0].reshape(ys, CORES, piece, ffw).transpose(1, 0, 2, 3)
    weight = weight.reshape(CORES, half, ffw)
    got_relay, both_acts, weight = lax.optimization_barrier((got_relay, both_acts, weight))

    halves = [
        jnp.concatenate(
            [
                got[:, ffw + c * DIRECT : ffw + (c + 1) * DIRECT],
                got_relay[:, c * relayed : (c + 1) * relayed],
            ],
            axis=1,
        )
        for c in range(CORES)
    ]
    mine = jnp.where(core == 0, halves[0], halves[1])
    theirs = jnp.where(core == 0, halves[1], halves[0])

    rows_dim = (((0,), (0,)), ((), ()))
    both_grads = jnp.concatenate([mine, lax.ppermute(theirs, "core", swap)], axis=0)
    partial_value = dot(both_grads, both_acts, rows_dim).astype(BF16)
    grad_down = lax.psum_scatter(partial_value, "y", scatter_dimension=0, tiled=True)

    projected = sum(dot(halves[c], weight[c]) for c in range(CORES)).astype(BF16)
    returned = exchange(
        projected.reshape(owners, 2, cap * ffw // 2), ("near", "x", "far")
    ).reshape(slots_here, ffw)
    back = dot(placing, returned, rows_dim).reshape(tok, topk, ffw)
    grad_hidden = (combine[:, :, None] * back).astype(BF16)
    grad_weights = jnp.sum(hidden.astype(F32) * back, axis=2)
    return (grad_hidden, grad_weights, grad_down[None])


def solution(mesh):
    dp, expert = mesh.shape["dp"], mesh.shape["expert"]
    shape = (dp // CORES, CORES, expert // (XS * PAIR), PAIR, XS)
    fine = Mesh(mesh.devices.reshape(shape), ("y", "core", "far", "near", "x"))
    tokens = ("y", "core", "far", "near", "x")
    owner = ("far", "near", "x")
    placed = (
        P(tokens, None),
        P(tokens, None, None),
        P(tokens, None),
        P(tokens, None),
        P(owner, None, None),
    )
    return jax.shard_map(
        local,
        mesh=fine,
        in_specs=placed,
        out_specs=(
            P(tokens, None, None),
            P(tokens, None),
            P(owner, ("y", "core"), None),
        ),
        check_vma=False,
    )
```

```python
import jax
import jax.numpy as jnp
from jax import lax
from jax.sharding import Mesh
from jax.sharding import PartitionSpec as P

CORES = 2
XS = 4
PAIR = 2
DIRECT = 128
F32 = jnp.float32
BF16 = jnp.bfloat16
ROWS = (((0,), (0,)), ((), ()))


def dot(a, b, dims=(((1,), (0,)), ((), ()))):
    return lax.dot_general(a, b, dims, preferred_element_type=F32)


def exchange(value, axes):
    return lax.all_to_all(value, axes, split_axis=0, concat_axis=0, tiled=True)


def local(out_grad, hidden, combine, expert_ids, down_weight):
    tok, width = out_grad.shape
    topk = expert_ids.shape[1]
    ffw = hidden.shape[2]
    xs, ys = lax.axis_size("x"), lax.axis_size("y")
    far, near = lax.axis_size("far"), lax.axis_size("near")
    core, far_here = lax.axis_index("core"), lax.axis_index("far")
    owners = far * near * xs
    plane = near * xs
    cap = min(tok, 3 * tok * topk // (2 * owners))
    rows = tok * topk
    slots_here = owners * cap
    half = width // CORES
    piece = half // ys

    flat_ids = expert_ids.reshape(rows)
    onehot = (flat_ids[:, None] == jnp.arange(owners, dtype=jnp.int32)[None, :]).astype(jnp.int32)
    before = jnp.cumsum(onehot, axis=0) - onehot
    slot = jnp.sum(onehot * before, axis=1)
    target = flat_ids * cap + slot
    all_slots = jnp.arange(slots_here, dtype=jnp.int32)[:, None]
    placing = (target[None, :] == all_slots).astype(BF16)
    weighted = (combine[:, :, None] * hidden.astype(F32)).astype(BF16).reshape(rows, ffw)

    by_core = (
        out_grad.reshape(tok, ys, CORES, piece).transpose(0, 2, 1, 3).reshape(tok, CORES, half)
    )
    direct = jnp.concatenate(
        [out_grad[:, c * piece : c * piece + DIRECT] for c in range(CORES)], axis=1
    )
    direct = jnp.broadcast_to(direct[:, None, :], (tok, topk, CORES * DIRECT))
    send = dot(
        placing, jnp.concatenate([weighted, direct.reshape(rows, CORES * DIRECT)], axis=1)
    ).astype(BF16)
    got = exchange(send.reshape(far, plane * cap, send.shape[1]), "far")

    slots_wide = jnp.pad(target.reshape(tok, topk).astype(BF16), ((0, 0), (0, 128 - topk)))
    gathered = lax.all_gather(
        jnp.concatenate([slots_wide, by_core[:, 0, DIRECT:], by_core[:, 1, DIRECT:]], axis=1),
        "far",
        axis=0,
        tiled=True,
    )

    row = jnp.arange(slots_here, dtype=jnp.int32)
    row_far = row // cap % far
    row_slot = (far_here * plane + row // (cap * far)) * cap + row % cap
    seen = gathered[:, :topk].astype(jnp.int32).T
    picking = jnp.any(seen[:, None, :] == row_slot[None, :, None], axis=0)
    column_far = jnp.arange(far * tok, dtype=jnp.int32) // tok
    picking = (picking & (row_far[:, None] == column_far[None, :])).astype(BF16)
    column = jnp.arange(slots_here, dtype=jnp.int32)
    turning = row_far * (plane * cap) + row // (cap * far) * cap + row % cap
    turning = (turning[:, None] == column[None, :]).astype(BF16)
    picking, got = lax.optimization_barrier((picking, got))
    near_rows = dot(turning, got.reshape(slots_here, ffw + CORES * DIRECT)).astype(BF16)
    relayed = half - DIRECT
    relay_send = jnp.stack(
        [
            jnp.concatenate(
                [
                    near_rows[:, ffw + c * DIRECT : ffw + (c + 1) * DIRECT],
                    dot(
                        picking, gathered[:, 128 + c * relayed : 128 + (c + 1) * relayed]
                    ).astype(BF16),
                    near_rows[:, :ffw],
                ],
                axis=1,
            )
            for c in range(CORES)
        ]
    )
    relay = exchange(
        relay_send.reshape(CORES * plane, far * cap, half + ffw), ("core", "near", "x")
    ).reshape(CORES * slots_here, half + ffw)

    weight = lax.dynamic_index_in_dim(
        down_weight[0].reshape(ys, CORES, piece, ffw), core, 1, keepdims=False
    ).reshape(half, ffw)
    relay, weight = lax.optimization_barrier((relay, weight))

    grads, acts = relay[:, :half], relay[:, half:]
    partial_value = dot(grads, acts, ROWS).astype(BF16)
    grad_down = lax.psum_scatter(partial_value, "y", scatter_dimension=0, tiled=True)

    halves = dot(grads, weight).reshape(CORES, slots_here, ffw)
    mine = lax.dynamic_index_in_dim(halves, core, 0, keepdims=False)
    theirs = lax.dynamic_index_in_dim(halves, 1 - core, 0, keepdims=False).astype(BF16)
    theirs = lax.ppermute(theirs, "core", [(0, 1), (1, 0)])
    projected = (mine + theirs.astype(F32)).astype(BF16)
    returned = exchange(
        projected.reshape(owners, 2, cap * ffw // 2), ("near", "x", "far")
    ).reshape(slots_here, ffw)
    back_target = (flat_ids % plane * far + flat_ids // plane) * cap + slot
    back_placing = (back_target[None, :] == all_slots).astype(BF16)
    back = dot(back_placing, returned, ROWS).reshape(tok, topk, ffw)
    grad_hidden = (combine[:, :, None] * back).astype(BF16)
    grad_weights = jnp.sum(hidden.astype(F32) * back, axis=2)
    return (grad_hidden, grad_weights, grad_down[None])


def solution(mesh):
    dp, expert = mesh.shape["dp"], mesh.shape["expert"]
    shape = (dp // CORES, CORES, expert // (XS * PAIR), PAIR, XS)
    fine = Mesh(mesh.devices.reshape(shape), ("y", "core", "far", "near", "x"))
    tokens = ("y", "core", "far", "near", "x")
    owner = ("far", "near", "x")
    placed = (
        P(tokens, None),
        P(tokens, None, None),
        P(tokens, None),
        P(tokens, None),
        P(owner, None, None),
    )
    return jax.shard_map(
        local,
        mesh=fine,
        in_specs=placed,
        out_specs=(
            P(tokens, None, None),
            P(tokens, None),
            P(owner, ("y", "core"), None),
        ),
        check_vma=False,
    )
```

```python
import functools

import jax
import jax.numpy as jnp
from jax import lax
from jax.experimental import pallas as pl
from jax.experimental.pallas import tpu as pltpu
from jax.sharding import Mesh
from jax.sharding import PartitionSpec as P

CORES = 2
XS = 4
PAIR = 2
DIRECT = 128
LANES = 128
F32 = jnp.float32
BF16 = jnp.bfloat16
ROWS = (((0,), (0,)), ((), ()))


def dot(a, b, dims=(((1,), (0,)), ((), ()))):
    return lax.dot_general(a, b, dims, preferred_element_type=F32)


def exchange(value, axes):
    return lax.all_to_all(value, axes, split_axis=0, concat_axis=0, tiled=True)


def over(number, by):
    return (number * (512 // by + 1)) >> 9


def iota(shape, dim):
    return lax.broadcasted_iota(jnp.int32, shape, dim)


def pack_kernel(owners, cap, pieces, owner_ref, combine_ref, hidden_ref, grad_ref, send_ref, pack_ref):
    topk, tok = owner_ref.shape
    pairs, ffw = hidden_ref.shape
    slots = owners * cap
    owner = owner_ref[...]
    wide = iota((LANES, tok), 0)
    names = sum((wide == owner[k : k + 1, :]).astype(F32) for k in range(topk))
    earlier = (iota((tok, tok), 0) < iota((tok, tok), 1)).astype(BF16)
    nth = dot(names.astype(BF16), earlier)
    row = iota((slots, LANES), 0)
    row_owner = over(row, cap)
    spread = (row_owner == iota((slots, LANES), 1)).astype(BF16)
    row_names = dot(spread, names.astype(BF16))
    row_nth = dot(spread, nth.astype(BF16))
    row_slot = (row - cap * row_owner).astype(F32)[:, :tok]
    by_token = ((row_names > 0) & (row_nth == row_slot)).astype(BF16)
    lane = iota((tok, pairs), 1)
    first = topk * iota((tok, pairs), 0)
    widen = ((lane >= first) & (lane < first + topk)).astype(BF16)
    own_k = (iota((topk, pairs), 1) & (topk - 1)) == iota((topk, pairs), 0)
    pair_owner = dot(owner.astype(F32).astype(BF16), widen)
    pair_owner = jnp.sum(jnp.where(own_k, pair_owner, 0.0), axis=0, keepdims=True)
    pair_combine = lax.dot_general(
        combine_ref[...],
        widen.astype(F32),
        (((1,), (0,)), ((), ())),
        precision=lax.Precision.HIGHEST,
        preferred_element_type=F32,
    )
    pair_combine = jnp.sum(jnp.where(own_k, pair_combine, 0.0), axis=0, keepdims=True)
    placing = jnp.where(row_owner.astype(F32) == pair_owner, dot(by_token, widen), 0.0)
    scale = jnp.sum(placing * pair_combine, axis=1, keepdims=True)
    send_ref[:, :ffw] = (dot(placing.astype(BF16), hidden_ref[...]) * scale).astype(BF16)
    piece = grad_ref.shape[1] // pieces
    for c in range(CORES):
        send_ref[:, ffw + c * DIRECT : ffw + (c + 1) * DIRECT] = dot(
            by_token, grad_ref[:, c * piece : c * piece + DIRECT]
        ).astype(BF16)
    numbers = (names * (nth + 1.0)).astype(BF16)
    same = (iota((tok, tok), 0) == iota((tok, tok), 1)).astype(BF16)
    pack_ref[:, :LANES] = dot(same, numbers, (((1,), (1,)), ((), ()))).astype(BF16)
    at = LANES
    for c in range(CORES):
        for y in range(pieces // CORES):
            start = (y * CORES + c) * piece
            skip = DIRECT if y == 0 else 0
            pack_ref[:, at : at + piece - skip] = grad_ref[:, start + skip : start + piece]
            at += piece - skip


def pick_kernel(far, plane, cap, far_ref, gathered_ref, out_ref):
    tokens = gathered_ref.shape[0]
    tok = tokens // far
    slots = plane * far * cap
    chosen = (iota((plane, LANES), 1) == far * iota((plane, LANES), 0) + far_ref[0]).astype(BF16)
    numbers = dot(chosen, gathered_ref[:, :LANES], (((1,), (1,)), ((), ())))
    row = iota((slots, tokens), 0)
    group = over(row, cap)
    slot = row - cap * group
    row_far, row_plane = group & (far - 1), group >> (far.bit_length() - 1)
    spread = (row_plane[:, :plane] == iota((slots, plane), 1)).astype(BF16)
    numbers = dot(spread, numbers.astype(BF16))
    column_far = iota((slots, tokens), 1) >> (tok.bit_length() - 1)
    picking = jnp.where(
        (column_far == row_far) & (numbers == (slot + 1).astype(F32)), 1.0, 0.0
    ).astype(BF16)
    step = 3 * LANES
    for at in range(0, out_ref.shape[1], step):
        out_ref[:, at : at + step] = dot(
            picking, gathered_ref[:, LANES + at : LANES + at + step]
        ).astype(BF16)


def local(out_grad, hidden, combine, expert_ids, down_weight):
    tok, width = out_grad.shape
    topk = expert_ids.shape[1]
    ffw = hidden.shape[2]
    xs, ys = lax.axis_size("x"), lax.axis_size("y")
    far, near = lax.axis_size("far"), lax.axis_size("near")
    core, far_here = lax.axis_index("core"), lax.axis_index("far")
    owners = far * near * xs
    plane = near * xs
    cap = min(tok, 3 * tok * topk // (2 * owners))
    rows = tok * topk
    slots_here = owners * cap
    half = width // CORES
    piece = half // ys
    relayed = half - DIRECT
    wide = ffw + CORES * DIRECT
    params = pltpu.CompilerParams(vmem_limit_bytes=32 << 20)

    owner = expert_ids % plane * far + expert_ids // plane
    send, pack = pl.pallas_call(
        functools.partial(pack_kernel, owners, cap, ys * CORES),
        out_shape=(
            jax.ShapeDtypeStruct((slots_here, wide), BF16),
            jax.ShapeDtypeStruct((tok, LANES + CORES * relayed), BF16),
        ),
        compiler_params=params,
        name="pack",
    )(owner.T, combine.T, hidden.reshape(rows, ffw), out_grad)
    got = exchange(
        send.reshape(owners, cap * wide // LANES, LANES), ("near", "x", "far")
    ).reshape(slots_here, wide)
    gathered = lax.all_gather(pack, "far", axis=0, tiled=True)

    gathered, got = lax.optimization_barrier((gathered, got))
    relay_rows = pl.pallas_call(
        functools.partial(pick_kernel, far, plane, cap),
        out_shape=jax.ShapeDtypeStruct((slots_here, CORES * relayed), BF16),
        in_specs=[
            pl.BlockSpec(memory_space=pltpu.SMEM),
            pl.BlockSpec(memory_space=pltpu.VMEM),
        ],
        compiler_params=params,
        name="pick",
    )(far_here.astype(jnp.int32).reshape(1), gathered)
    got_relay = exchange(
        relay_rows.reshape(plane, far * cap, CORES * relayed), ("near", "x")
    ).reshape(slots_here, CORES * relayed)

    swap = [(0, 1), (1, 0)]
    acts = got[:, :ffw]
    both_acts = jnp.concatenate([acts, lax.ppermute(acts, "core", swap)], axis=0)
    weight = down_weight[0].reshape(ys, CORES, piece, ffw).transpose(1, 0, 2, 3)
    weight = weight.reshape(CORES, half, ffw)
    got_relay, both_acts, weight = lax.optimization_barrier((got_relay, both_acts, weight))

    halves = [
        jnp.concatenate(
            [
                got[:, ffw + c * DIRECT : ffw + (c + 1) * DIRECT],
                got_relay[:, c * relayed : (c + 1) * relayed],
            ],
            axis=1,
        )
        for c in range(CORES)
    ]
    mine = jnp.where(core == 0, halves[0], halves[1])
    theirs = jnp.where(core == 0, halves[1], halves[0])

    both_grads = jnp.concatenate([mine, lax.ppermute(theirs, "core", swap)], axis=0)
    partial_value = dot(both_grads, both_acts, ROWS).astype(BF16)
    grad_down = lax.psum_scatter(partial_value, "y", scatter_dimension=0, tiled=True)

    projected = sum(dot(halves[c], weight[c]) for c in range(CORES)).astype(BF16)
    returned = exchange(
        projected.reshape(owners, 2, cap * ffw // 2), ("near", "x", "far")
    ).reshape(slots_here, ffw)
    slots = owner.reshape(rows)
    onehot = (slots[:, None] == jnp.arange(owners, dtype=jnp.int32)[None, :]).astype(jnp.int32)
    before = jnp.cumsum(onehot, axis=0) - onehot
    slots = slots * cap + jnp.sum(onehot * before, axis=1)
    placing = slots[None, :] == jnp.arange(slots_here, dtype=jnp.int32)[:, None]
    back = dot(placing.astype(BF16), returned, ROWS).reshape(tok, topk, ffw)
    grad_hidden = (combine[:, :, None] * back).astype(BF16)
    grad_weights = jnp.sum(hidden.astype(F32) * back, axis=2)
    return (grad_hidden, grad_weights, grad_down[None])


def solution(mesh):
    dp, expert = mesh.shape["dp"], mesh.shape["expert"]
    shape = (dp // CORES, CORES, expert // (XS * PAIR), PAIR, XS)
    fine = Mesh(mesh.devices.reshape(shape), ("y", "core", "far", "near", "x"))
    tokens = ("y", "core", "far", "near", "x")
    owner = ("far", "near", "x")
    placed = (
        P(tokens, None),
        P(tokens, None, None),
        P(tokens, None),
        P(tokens, None),
        P(owner, None, None),
    )
    return jax.shard_map(
        local,
        mesh=fine,
        in_specs=placed,
        out_specs=(
            P(tokens, None, None),
            P(tokens, None),
            P(owner, ("y", "core"), None),
        ),
        check_vma=False,
    )
```

```python
import functools

import jax
import jax.numpy as jnp
from jax import lax
from jax.experimental import pallas as pl
from jax.experimental.pallas import tpu as pltpu
from jax.sharding import Mesh
from jax.sharding import PartitionSpec as P

CORES = 2
XS = 4
PAIR = 2
DIRECT = 128
PACK_LIMIT = 56 << 20
LANES = 128
F32 = jnp.float32
BF16 = jnp.bfloat16
ROWS = (((0,), (0,)), ((), ()))


def dot(a, b, dims=(((1,), (0,)), ((), ()))):
    return lax.dot_general(a, b, dims, preferred_element_type=F32)


def exchange(value, axes):
    return lax.all_to_all(value, axes, split_axis=0, concat_axis=0, tiled=True)


def over(number, by):
    return (number * (512 // by + 1)) >> 9


def iota(shape, dim):
    return lax.broadcasted_iota(jnp.int32, shape, dim)


def pack_kernel(owners, cap, plane, pieces, *refs):
    sources, (send_ref, pack_ref), inside = refs[:4], refs[4:6], refs[6:10]
    tall_ref, sems = refs[10:]
    copies = [
        pltpu.make_async_copy(source, target, sems.at[i])
        for i, (source, target) in enumerate(zip(sources, inside))
    ]
    for copy in copies:
        copy.start()
    for copy in copies:
        copy.wait()
    ids_ref, combine_ref, hidden_ref, grad_ref = inside
    topk, tok = ids_ref.shape
    pairs, ffw = hidden_ref.shape
    slots = owners * cap
    ids = ids_ref[...]
    owner = (ids & (plane - 1)) * (owners // plane) + (ids >> (plane.bit_length() - 1))
    wide = iota((LANES, tok), 0)
    names = sum((wide == owner[k : k + 1, :]).astype(F32) for k in range(topk))
    earlier = (iota((tok, tok), 0) < iota((tok, tok), 1)).astype(BF16)
    nth = dot(names.astype(BF16), earlier)
    row = iota((slots, LANES), 0)
    row_owner = over(row, cap)
    spread = (row_owner == iota((slots, LANES), 1)).astype(BF16)
    row_names = dot(spread, names.astype(BF16))
    row_nth = dot(spread, nth.astype(BF16))
    row_slot = (row - cap * row_owner).astype(F32)[:, :tok]
    by_token = ((row_names > 0) & (row_nth == row_slot)).astype(BF16)
    lane = iota((tok, pairs), 1)
    first = topk * iota((tok, pairs), 0)
    widen = ((lane >= first) & (lane < first + topk)).astype(BF16)
    own_k = (iota((topk, pairs), 1) & (topk - 1)) == iota((topk, pairs), 0)
    pair_owner = dot(owner.astype(F32).astype(BF16), widen)
    pair_owner = jnp.sum(jnp.where(own_k, pair_owner, 0.0), axis=0, keepdims=True)
    pair_combine = lax.dot_general(
        combine_ref[...],
        widen.astype(F32),
        (((1,), (0,)), ((), ())),
        precision=lax.Precision.HIGHEST,
        preferred_element_type=F32,
    )
    pair_combine = jnp.sum(jnp.where(own_k, pair_combine, 0.0), axis=0, keepdims=True)
    placing = jnp.where(row_owner.astype(F32) == pair_owner, dot(by_token, widen), 0.0)
    scale = jnp.sum(placing * pair_combine, axis=1, keepdims=True)
    piece = grad_ref.shape[1] // pieces
    acts = dot(placing.astype(BF16), hidden_ref[...]) * scale
    direct = [
        dot(by_token, grad_ref[:, c * piece : c * piece + DIRECT]) for c in range(CORES)
    ]
    blocks = [acts[:, at : at + LANES] for at in range(0, ffw, LANES)] + direct
    for i, block in enumerate(blocks):
        tall_ref[pl.ds(i, slots, stride=len(blocks)), :] = block
    send_ref[...] = tall_ref[...].astype(BF16)
    numbers = (names * (nth + 1.0)).astype(BF16)
    same = (iota((tok, tok), 0) == iota((tok, tok), 1)).astype(BF16)
    pack_ref[:, :LANES] = dot(same, numbers, (((1,), (1,)), ((), ()))).astype(BF16)
    at = LANES
    for c in range(CORES):
        for y in range(pieces // CORES):
            start = (y * CORES + c) * piece
            skip = DIRECT if y == 0 else 0
            pack_ref[:, at : at + piece - skip] = grad_ref[:, start + skip : start + piece]
            at += piece - skip


def pick_kernel(far, plane, cap, far_ref, gathered_ref, out_ref):
    tokens = gathered_ref.shape[0]
    tok = tokens // far
    slots = plane * far * cap
    chosen = (iota((plane, LANES), 1) == far * iota((plane, LANES), 0) + far_ref[0]).astype(BF16)
    numbers = dot(chosen, gathered_ref[:, :LANES], (((1,), (1,)), ((), ())))
    row = iota((slots, tokens), 0)
    group = over(row, cap)
    slot = row - cap * group
    row_far, row_plane = group & (far - 1), group >> (far.bit_length() - 1)
    spread = (row_plane[:, :plane] == iota((slots, plane), 1)).astype(BF16)
    numbers = dot(spread, numbers.astype(BF16))
    column_far = iota((slots, tokens), 1) >> (tok.bit_length() - 1)
    picking = jnp.where(
        (column_far == row_far) & (numbers == (slot + 1).astype(F32)), 1.0, 0.0
    ).astype(BF16)
    columns, step = out_ref.shape[2], 3 * LANES
    for c in range(CORES):
        for at in range(0, columns, step):
            start = LANES + c * columns + at
            out_ref[c, :, at : at + step] = dot(
                picking, gathered_ref[:, start : start + step]
            ).astype(BF16)


def local(out_grad, hidden, combine, expert_ids, down_weight):
    tok, width = out_grad.shape
    topk = expert_ids.shape[1]
    ffw = hidden.shape[2]
    xs, ys = lax.axis_size("x"), lax.axis_size("y")
    far, near = lax.axis_size("far"), lax.axis_size("near")
    core, far_here = lax.axis_index("core"), lax.axis_index("far")
    owners = far * near * xs
    plane = near * xs
    cap = min(tok, 3 * tok * topk // (2 * owners))
    rows = tok * topk
    slots_here = owners * cap
    half = width // CORES
    piece = half // ys
    relayed = half - DIRECT
    wide = ffw + CORES * DIRECT
    params = pltpu.CompilerParams(vmem_limit_bytes=32 << 20)

    tall = slots_here * wide // LANES
    send, pack = pl.pallas_call(
        functools.partial(pack_kernel, owners, cap, plane, ys * CORES),
        out_shape=(
            jax.ShapeDtypeStruct((tall, LANES), BF16),
            jax.ShapeDtypeStruct((tok, LANES + CORES * relayed), BF16),
        ),
        in_specs=[pl.BlockSpec(memory_space=pl.ANY)] * 4,
        scratch_shapes=[
            pltpu.VMEM((topk, tok), jnp.int32),
            pltpu.VMEM((topk, tok), F32),
            pltpu.VMEM((rows, ffw), BF16),
            pltpu.VMEM((tok, width), BF16),
            pltpu.VMEM((tall, LANES), F32),
            pltpu.SemaphoreType.DMA((4,)),
        ],
        compiler_params=pltpu.CompilerParams(vmem_limit_bytes=PACK_LIMIT),
        name="pack",
    )(expert_ids.T, combine.T, hidden.reshape(rows, ffw), out_grad)
    got = exchange(
        send.reshape(owners, cap * wide // LANES, LANES), ("near", "x", "far")
    ).reshape(slots_here, wide)
    gathered = lax.all_gather(pack, "far", axis=0, tiled=True)

    gathered, got = lax.optimization_barrier((gathered, got))
    relay_rows = pl.pallas_call(
        functools.partial(pick_kernel, far, plane, cap),
        out_shape=jax.ShapeDtypeStruct((CORES, slots_here, relayed), BF16),
        in_specs=[
            pl.BlockSpec(memory_space=pltpu.SMEM),
            pl.BlockSpec(memory_space=pltpu.VMEM),
        ],
        compiler_params=params,
        name="pick",
    )(far_here.astype(jnp.int32).reshape(1), gathered)
    relay = exchange(
        relay_rows.reshape(CORES * plane, far * cap, relayed), ("core", "near", "x")
    ).reshape(CORES * slots_here, relayed)

    swap = [(0, 1), (1, 0)]
    acts, sides = got[:, :ffw], (got[:, ffw : ffw + DIRECT], got[:, ffw + DIRECT :])
    own, out = [jnp.where(core == 0, sides[c], sides[1 - c]) for c in range(CORES)]
    own = jnp.concatenate([acts, own], axis=1)
    other = lax.ppermute(jnp.concatenate([acts, out], axis=1), "core", swap)
    both = jnp.concatenate(
        [jnp.where(core == 0, own, other), jnp.where(core == 0, other, own)], axis=0
    )
    weight = lax.dynamic_index_in_dim(
        down_weight[0].reshape(ys, CORES, piece, ffw), core, 1, keepdims=False
    ).reshape(half, ffw)
    relay, both, weight = lax.optimization_barrier((relay, both, weight))

    grads = jnp.concatenate([both[:, ffw:], relay], axis=1)
    partial_value = dot(grads, both[:, :ffw], ROWS).astype(BF16)
    grad_down = lax.psum_scatter(partial_value, "y", scatter_dimension=0, tiled=True)

    halves = dot(grads, weight).reshape(CORES, slots_here, ffw)
    mine = lax.dynamic_index_in_dim(halves, core, 0, keepdims=False)
    theirs = lax.dynamic_index_in_dim(halves, 1 - core, 0, keepdims=False).astype(BF16)
    projected = (mine + lax.ppermute(theirs, "core", swap).astype(F32)).astype(BF16)
    returned = exchange(
        projected.reshape(owners, 2, cap * ffw // 2), ("near", "x", "far")
    ).reshape(slots_here, ffw)
    slots = (expert_ids % plane * far + expert_ids // plane).reshape(rows)
    onehot = (slots[:, None] == jnp.arange(owners, dtype=jnp.int32)[None, :]).astype(jnp.int32)
    before = jnp.cumsum(onehot, axis=0) - onehot
    slots = slots * cap + jnp.sum(onehot * before, axis=1)
    placing = slots[None, :] == jnp.arange(slots_here, dtype=jnp.int32)[:, None]
    back = dot(placing.astype(BF16), returned, ROWS).reshape(tok, topk, ffw)
    grad_hidden = (combine[:, :, None] * back).astype(BF16)
    grad_weights = jnp.sum(hidden.astype(F32) * back, axis=2)
    return (grad_hidden, grad_weights, grad_down[None])


def solution(mesh):
    dp, expert = mesh.shape["dp"], mesh.shape["expert"]
    shape = (dp // CORES, CORES, expert // (XS * PAIR), PAIR, XS)
    fine = Mesh(mesh.devices.reshape(shape), ("y", "core", "far", "near", "x"))
    tokens = ("y", "core", "far", "near", "x")
    owner = ("far", "near", "x")
    placed = (
        P(tokens, None),
        P(tokens, None, None),
        P(tokens, None),
        P(tokens, None),
        P(owner, None, None),
    )
    return jax.shard_map(
        local,
        mesh=fine,
        in_specs=placed,
        out_specs=(
            P(tokens, None, None),
            P(tokens, None),
            P(owner, ("y", "core"), None),
        ),
        check_vma=False,
    )
```

```python
import functools

import jax
import jax.numpy as jnp
from jax import lax
from jax.experimental import pallas as pl
from jax.experimental.pallas import tpu as pltpu
from jax.sharding import Mesh
from jax.sharding import PartitionSpec as P

CORES = 2
XS = 4
PAIR = 2
DIRECT = 128
PACK_LIMIT = 56 << 20
LANES = 128
F32 = jnp.float32
BF16 = jnp.bfloat16
ROWS = (((0,), (0,)), ((), ()))


def dot(a, b, dims=(((1,), (0,)), ((), ()))):
    return lax.dot_general(a, b, dims, preferred_element_type=F32)


def exchange(value, axes):
    return lax.all_to_all(value, axes, split_axis=0, concat_axis=0, tiled=True)


def over(number, by):
    return (number * (512 // by + 1)) >> 9


def iota(shape, dim):
    return lax.broadcasted_iota(jnp.int32, shape, dim)


def pack_kernel(owners, cap, plane, pieces, *refs):
    sources, (send_ref, pack_ref, direct_ref), inside = refs[:4], refs[4:7], refs[7:11]
    sems = refs[11]
    copies = [
        pltpu.make_async_copy(source, target, sems.at[i])
        for i, (source, target) in enumerate(zip(sources, inside))
    ]
    for copy in copies:
        copy.start()
    for copy in copies:
        copy.wait()
    ids_ref, combine_ref, hidden_ref, grad_ref = inside
    topk, tok = ids_ref.shape
    pairs, ffw = hidden_ref.shape
    slots = owners * cap
    ids = ids_ref[...]
    owner = (ids & (plane - 1)) * (owners // plane) + (ids >> (plane.bit_length() - 1))
    wide = iota((LANES, tok), 0)
    names = sum((wide == owner[k : k + 1, :]).astype(F32) for k in range(topk))
    earlier = (iota((tok, tok), 0) < iota((tok, tok), 1)).astype(BF16)
    nth = dot(names.astype(BF16), earlier)
    row = iota((slots, LANES), 0)
    row_owner = over(row, cap)
    spread = (row_owner == iota((slots, LANES), 1)).astype(BF16)
    row_names = dot(spread, names.astype(BF16))
    row_nth = dot(spread, nth.astype(BF16))
    row_slot = (row - cap * row_owner).astype(F32)[:, :tok]
    by_token = ((row_names > 0) & (row_nth == row_slot)).astype(BF16)
    lane = iota((tok, pairs), 1)
    first = topk * iota((tok, pairs), 0)
    widen = ((lane >= first) & (lane < first + topk)).astype(BF16)
    own_k = (iota((topk, pairs), 1) & (topk - 1)) == iota((topk, pairs), 0)
    pair_owner = dot(owner.astype(F32).astype(BF16), widen)
    pair_owner = jnp.sum(jnp.where(own_k, pair_owner, 0.0), axis=0, keepdims=True)
    pair_combine = lax.dot_general(
        combine_ref[...],
        widen.astype(F32),
        (((1,), (0,)), ((), ())),
        precision=lax.Precision.HIGHEST,
        preferred_element_type=F32,
    )
    pair_combine = jnp.sum(jnp.where(own_k, pair_combine, 0.0), axis=0, keepdims=True)
    placing = jnp.where(row_owner.astype(F32) == pair_owner, dot(by_token, widen), 0.0)
    scale = jnp.sum(placing * pair_combine, axis=1, keepdims=True)
    piece = grad_ref.shape[1] // pieces
    send_ref[...] = (dot(placing.astype(BF16), hidden_ref[...]) * scale).astype(BF16)
    for c in range(CORES):
        direct_ref[:, c * DIRECT : (c + 1) * DIRECT] = grad_ref[:, c * piece : c * piece + DIRECT]
    numbers = (names * (nth + 1.0)).astype(BF16)
    same = (iota((tok, tok), 0) == iota((tok, tok), 1)).astype(BF16)
    pack_ref[:, :LANES] = dot(same, numbers, (((1,), (1,)), ((), ()))).astype(BF16)
    at = LANES
    for c in range(CORES):
        for y in range(pieces // CORES):
            start = (y * CORES + c) * piece
            skip = DIRECT if y == 0 else 0
            pack_ref[:, at : at + piece - skip] = grad_ref[:, start + skip : start + piece]
            at += piece - skip


def pick_kernel(far, plane, cap, far_ref, gathered_ref, direct_ref, out_ref):
    tokens = gathered_ref.shape[0]
    tok = tokens // far
    slots = plane * far * cap
    chosen = (iota((plane, LANES), 1) == far * iota((plane, LANES), 0) + far_ref[0]).astype(BF16)
    numbers = dot(chosen, gathered_ref[:, :LANES], (((1,), (1,)), ((), ())))
    row = iota((slots, tokens), 0)
    group = over(row, cap)
    slot = row - cap * group
    row_far, row_plane = group & (far - 1), group >> (far.bit_length() - 1)
    spread = (row_plane[:, :plane] == iota((slots, plane), 1)).astype(BF16)
    numbers = dot(spread, numbers.astype(BF16))
    column_far = iota((slots, tokens), 1) >> (tok.bit_length() - 1)
    picking = jnp.where(
        (column_far == row_far) & (numbers == (slot + 1).astype(F32)), 1.0, 0.0
    ).astype(BF16)
    half, step = out_ref.shape[1] // CORES, 3 * LANES
    for c in range(CORES):
        out_ref[:, c * half : c * half + DIRECT] = dot(
            picking, direct_ref[:, c * DIRECT : (c + 1) * DIRECT]
        ).astype(BF16)
        for at in range(0, half - DIRECT, step):
            start, to = LANES + c * (half - DIRECT) + at, c * half + DIRECT + at
            out_ref[:, to : to + step] = dot(
                picking, gathered_ref[:, start : start + step]
            ).astype(BF16)


def local(out_grad, hidden, combine, expert_ids, down_weight):
    tok, width = out_grad.shape
    topk = expert_ids.shape[1]
    ffw = hidden.shape[2]
    xs, ys = lax.axis_size("x"), lax.axis_size("y")
    far, near = lax.axis_size("far"), lax.axis_size("near")
    core, far_here = lax.axis_index("core"), lax.axis_index("far")
    owners = far * near * xs
    plane = near * xs
    cap = min(tok, 3 * tok * topk // (2 * owners))
    rows = tok * topk
    slots_here = owners * cap
    half = width // CORES
    piece = half // ys
    relayed = half - DIRECT
    params = pltpu.CompilerParams(vmem_limit_bytes=32 << 20)

    send, pack, direct = pl.pallas_call(
        functools.partial(pack_kernel, owners, cap, plane, ys * CORES),
        out_shape=(
            jax.ShapeDtypeStruct((slots_here, ffw), BF16),
            jax.ShapeDtypeStruct((tok, LANES + CORES * relayed), BF16),
            jax.ShapeDtypeStruct((tok, CORES * DIRECT), BF16),
        ),
        in_specs=[pl.BlockSpec(memory_space=pl.ANY)] * 4,
        scratch_shapes=[
            pltpu.VMEM((topk, tok), jnp.int32),
            pltpu.VMEM((topk, tok), F32),
            pltpu.VMEM((rows, ffw), BF16),
            pltpu.VMEM((tok, width), BF16),
            pltpu.SemaphoreType.DMA((4,)),
        ],
        compiler_params=pltpu.CompilerParams(vmem_limit_bytes=PACK_LIMIT),
        name="pack",
    )(expert_ids.T, combine.T, hidden.reshape(rows, ffw), out_grad)
    at_far = jnp.arange(far, dtype=jnp.int32)[:, None, None] == far_here
    direct = lax.psum(jnp.where(at_far, direct[None], jnp.zeros((), BF16)), "far")
    direct = direct.reshape(far * tok, CORES * DIRECT)
    acts = exchange(
        send.reshape(owners, 2, cap * ffw // 2), ("near", "x", "far")
    ).reshape(slots_here, ffw)
    gathered = lax.all_gather(pack, "far", axis=0, tiled=True)

    gathered, acts = lax.optimization_barrier((gathered, acts))
    relay_rows = pl.pallas_call(
        functools.partial(pick_kernel, far, plane, cap),
        out_shape=jax.ShapeDtypeStruct((slots_here, width), BF16),
        in_specs=[
            pl.BlockSpec(memory_space=pltpu.SMEM),
            pl.BlockSpec(memory_space=pltpu.VMEM),
            pl.BlockSpec(memory_space=pltpu.VMEM),
        ],
        compiler_params=params,
        name="pick",
    )(far_here.astype(jnp.int32).reshape(1), gathered, direct)
    relay = exchange(
        relay_rows.reshape(plane, far * cap, width), ("near", "x")
    ).reshape(slots_here, width)

    swap = [(0, 1), (1, 0)]
    both_acts = jnp.concatenate([acts, lax.ppermute(acts, "core", swap)], axis=0)
    weight = down_weight[0].reshape(ys, CORES, piece, ffw).transpose(1, 0, 2, 3)
    weight = weight.reshape(width, ffw)
    relay, both_acts, weight = lax.optimization_barrier((relay, both_acts, weight))

    sides = relay[:, :half], relay[:, half:]
    mine, theirs = [jnp.where(core == 0, sides[c], sides[1 - c]) for c in range(CORES)]
    both_grads = jnp.concatenate([mine, lax.ppermute(theirs, "core", swap)], axis=0)
    partial_value = dot(both_grads, both_acts, ROWS).astype(BF16)
    grad_down = lax.psum_scatter(partial_value, "y", scatter_dimension=0, tiled=True)

    projected = dot(relay, weight).astype(BF16)
    returned = exchange(
        projected.reshape(owners, 2, cap * ffw // 2), ("near", "x", "far")
    ).reshape(slots_here, ffw)
    slots = (expert_ids % plane * far + expert_ids // plane).reshape(rows)
    onehot = (slots[:, None] == jnp.arange(owners, dtype=jnp.int32)[None, :]).astype(jnp.int32)
    before = jnp.cumsum(onehot, axis=0) - onehot
    slots = slots * cap + jnp.sum(onehot * before, axis=1)
    placing = slots[None, :] == jnp.arange(slots_here, dtype=jnp.int32)[:, None]
    back = dot(placing.astype(BF16), returned, ROWS).reshape(tok, topk, ffw)
    grad_hidden = (combine[:, :, None] * back).astype(BF16)
    grad_weights = jnp.sum(hidden.astype(F32) * back, axis=2)
    return (grad_hidden, grad_weights, grad_down[None])


def solution(mesh):
    dp, expert = mesh.shape["dp"], mesh.shape["expert"]
    shape = (dp // CORES, CORES, expert // (XS * PAIR), PAIR, XS)
    fine = Mesh(mesh.devices.reshape(shape), ("y", "core", "far", "near", "x"))
    tokens = ("y", "core", "far", "near", "x")
    owner = ("far", "near", "x")
    placed = (
        P(tokens, None),
        P(tokens, None, None),
        P(tokens, None),
        P(tokens, None),
        P(owner, None, None),
    )
    return jax.shard_map(
        local,
        mesh=fine,
        in_specs=placed,
        out_specs=(
            P(tokens, None, None),
            P(tokens, None),
            P(owner, ("y", "core"), None),
        ),
        check_vma=False,
    )
```

```python
import functools

import jax
import jax.numpy as jnp
from jax import lax
from jax.experimental import pallas as pl
from jax.experimental.pallas import tpu as pltpu
from jax.sharding import Mesh
from jax.sharding import PartitionSpec as P

CORES = 2
XS = 4
PAIR = 2
DIRECT = 128
PACK_LIMIT = 56 << 20
LANES = 128
F32 = jnp.float32
BF16 = jnp.bfloat16
ROWS = (((0,), (0,)), ((), ()))


def dot(a, b, dims=(((1,), (0,)), ((), ()))):
    return lax.dot_general(a, b, dims, preferred_element_type=F32)


def exchange(value, axes):
    return lax.all_to_all(value, axes, split_axis=0, concat_axis=0, tiled=True)


def over(number, by):
    return (number * (512 // by + 1)) >> 9


def iota(shape, dim):
    return lax.broadcasted_iota(jnp.int32, shape, dim)


def pack_kernel(owners, cap, plane, pieces, *refs):
    sources, (send_ref, pack_ref), inside = refs[:4], refs[4:6], refs[6:10]
    tall_ref, sems = refs[10:]
    copies = [
        pltpu.make_async_copy(source, target, sems.at[i])
        for i, (source, target) in enumerate(zip(sources, inside))
    ]
    for copy in copies:
        copy.start()
    for copy in copies:
        copy.wait()
    ids_ref, combine_ref, hidden_ref, grad_ref = inside
    topk, tok = ids_ref.shape
    pairs, ffw = hidden_ref.shape
    slots = owners * cap
    ids = ids_ref[...]
    owner = (ids & (plane - 1)) * (owners // plane) + (ids >> (plane.bit_length() - 1))
    wide = iota((LANES, tok), 0)
    names = sum((wide == owner[k : k + 1, :]).astype(F32) for k in range(topk))
    earlier = (iota((tok, tok), 0) < iota((tok, tok), 1)).astype(BF16)
    nth = dot(names.astype(BF16), earlier)
    row = iota((slots, LANES), 0)
    row_owner = over(row, cap)
    spread = (row_owner == iota((slots, LANES), 1)).astype(BF16)
    row_names = dot(spread, names.astype(BF16))
    row_nth = dot(spread, nth.astype(BF16))
    row_slot = (row - cap * row_owner).astype(F32)[:, :tok]
    by_token = ((row_names > 0) & (row_nth == row_slot)).astype(BF16)
    lane = iota((tok, pairs), 1)
    first = topk * iota((tok, pairs), 0)
    widen = ((lane >= first) & (lane < first + topk)).astype(BF16)
    own_k = (iota((topk, pairs), 1) & (topk - 1)) == iota((topk, pairs), 0)
    pair_owner = dot(owner.astype(F32).astype(BF16), widen)
    pair_owner = jnp.sum(jnp.where(own_k, pair_owner, 0.0), axis=0, keepdims=True)
    pair_combine = lax.dot_general(
        combine_ref[...],
        widen.astype(F32),
        (((1,), (0,)), ((), ())),
        precision=lax.Precision.HIGHEST,
        preferred_element_type=F32,
    )
    pair_combine = jnp.sum(jnp.where(own_k, pair_combine, 0.0), axis=0, keepdims=True)
    placing = jnp.where(row_owner.astype(F32) == pair_owner, dot(by_token, widen), 0.0)
    scale = jnp.sum(placing * pair_combine, axis=1, keepdims=True)
    piece = grad_ref.shape[1] // pieces
    acts = dot(placing.astype(BF16), hidden_ref[...]) * scale
    direct = [
        dot(by_token, grad_ref[:, c * piece : c * piece + DIRECT]) for c in range(CORES)
    ]
    blocks = [acts[:, at : at + LANES] for at in range(0, ffw, LANES)] + direct
    for i, block in enumerate(blocks):
        tall_ref[pl.ds(i, slots, stride=len(blocks)), :] = block
    send_ref[...] = tall_ref[...].astype(BF16)
    numbers = (names * (nth + 1.0)).astype(BF16)
    same = (iota((tok, tok), 0) == iota((tok, tok), 1)).astype(BF16)
    pack_ref[:, :LANES] = dot(same, numbers, (((1,), (1,)), ((), ()))).astype(BF16)
    at = LANES
    for c in range(CORES):
        for y in range(pieces // CORES):
            start = (y * CORES + c) * piece
            skip = DIRECT if y == 0 else 0
            pack_ref[:, at : at + piece - skip] = grad_ref[:, start + skip : start + piece]
            at += piece - skip


def pick_kernel(far, plane, cap, far_ref, gathered_ref, out_ref):
    tokens = gathered_ref.shape[0]
    tok = tokens // far
    slots = plane * far * cap
    chosen = (iota((plane, LANES), 1) == far * iota((plane, LANES), 0) + far_ref[0]).astype(BF16)
    numbers = dot(chosen, gathered_ref[:, :LANES], (((1,), (1,)), ((), ())))
    row = iota((slots, tokens), 0)
    group = over(row, cap)
    slot = row - cap * group
    row_far, row_plane = group & (far - 1), group >> (far.bit_length() - 1)
    spread = (row_plane[:, :plane] == iota((slots, plane), 1)).astype(BF16)
    numbers = dot(spread, numbers.astype(BF16))
    column_far = iota((slots, tokens), 1) >> (tok.bit_length() - 1)
    picking = jnp.where(
        (column_far == row_far) & (numbers == (slot + 1).astype(F32)), 1.0, 0.0
    ).astype(BF16)
    step = 3 * LANES
    for at in range(0, out_ref.shape[1], step):
        out_ref[:, at : at + step] = dot(
            picking, gathered_ref[:, LANES + at : LANES + at + step]
        ).astype(BF16)


def local(out_grad, hidden, combine, expert_ids, down_weight):
    tok, width = out_grad.shape
    topk = expert_ids.shape[1]
    ffw = hidden.shape[2]
    xs, ys = lax.axis_size("x"), lax.axis_size("y")
    far, near = lax.axis_size("far"), lax.axis_size("near")
    core, far_here = lax.axis_index("core"), lax.axis_index("far")
    owners = far * near * xs
    plane = near * xs
    cap = min(tok, 3 * tok * topk // (2 * owners))
    rows = tok * topk
    slots_here = owners * cap
    half = width // CORES
    piece = half // ys
    relayed = half - DIRECT
    wide = ffw + CORES * DIRECT
    params = pltpu.CompilerParams(vmem_limit_bytes=32 << 20)

    tall = slots_here * wide // LANES
    send, pack = pl.pallas_call(
        functools.partial(pack_kernel, owners, cap, plane, ys * CORES),
        out_shape=(
            jax.ShapeDtypeStruct((tall, LANES), BF16),
            jax.ShapeDtypeStruct((tok, LANES + CORES * relayed), BF16),
        ),
        in_specs=[pl.BlockSpec(memory_space=pl.ANY)] * 4,
        scratch_shapes=[
            pltpu.VMEM((topk, tok), jnp.int32),
            pltpu.VMEM((topk, tok), F32),
            pltpu.VMEM((rows, ffw), BF16),
            pltpu.VMEM((tok, width), BF16),
            pltpu.VMEM((tall, LANES), F32),
            pltpu.SemaphoreType.DMA((4,)),
        ],
        compiler_params=pltpu.CompilerParams(vmem_limit_bytes=PACK_LIMIT),
        name="pack",
    )(expert_ids.T, combine.T, hidden.reshape(rows, ffw), out_grad)
    got = exchange(
        send.reshape(owners, cap * wide // LANES, LANES), ("near", "x", "far")
    ).reshape(slots_here, wide)
    gathered = lax.all_gather(pack, "far", axis=0, tiled=True)

    gathered, got = lax.optimization_barrier((gathered, got))
    relay_rows = pl.pallas_call(
        functools.partial(pick_kernel, far, plane, cap),
        out_shape=jax.ShapeDtypeStruct((slots_here, CORES * relayed), BF16),
        in_specs=[
            pl.BlockSpec(memory_space=pltpu.SMEM),
            pl.BlockSpec(memory_space=pltpu.VMEM),
        ],
        compiler_params=params,
        name="pick",
    )(far_here.astype(jnp.int32).reshape(1), gathered)
    relay = exchange(
        relay_rows.reshape(plane, far * cap, CORES * relayed), ("near", "x")
    ).reshape(slots_here, CORES * relayed)

    swap = [(0, 1), (1, 0)]
    acts = got[:, :ffw]
    both_acts = jnp.concatenate([acts, lax.ppermute(acts, "core", swap)], axis=0)
    weight = down_weight[0].reshape(ys, CORES, piece, ffw).transpose(1, 0, 2, 3)
    weight = weight.reshape(width, ffw)
    relay, both_acts, weight = lax.optimization_barrier((relay, both_acts, weight))

    halves = [
        jnp.concatenate(
            [
                got[:, ffw + c * DIRECT : ffw + (c + 1) * DIRECT],
                relay[:, c * relayed : (c + 1) * relayed],
            ],
            axis=1,
        )
        for c in range(CORES)
    ]
    mine, theirs = [jnp.where(core == 0, halves[c], halves[1 - c]) for c in range(CORES)]
    both_grads = jnp.concatenate([mine, lax.ppermute(theirs, "core", swap)], axis=0)
    part = ffw // 2
    grad_down = jnp.concatenate(
        [
            lax.psum_scatter(
                dot(both_grads, both_acts[:, at : at + part], ROWS).astype(BF16),
                "y",
                scatter_dimension=0,
                tiled=True,
            )
            for at in range(0, ffw, part)
        ],
        axis=1,
    )

    projected = (dot(halves[0], weight[:half]) + dot(halves[1], weight[half:])).astype(BF16)
    returned = exchange(
        projected.reshape(owners, 2, cap * ffw // 2), ("near", "x", "far")
    ).reshape(slots_here, ffw)
    slots = (expert_ids % plane * far + expert_ids // plane).reshape(rows)
    onehot = (slots[:, None] == jnp.arange(owners, dtype=jnp.int32)[None, :]).astype(jnp.int32)
    before = jnp.cumsum(onehot, axis=0) - onehot
    slots = slots * cap + jnp.sum(onehot * before, axis=1)
    placing = slots[None, :] == jnp.arange(slots_here, dtype=jnp.int32)[:, None]
    back = dot(placing.astype(BF16), returned, ROWS).reshape(tok, topk, ffw)
    grad_hidden = (combine[:, :, None] * back).astype(BF16)
    grad_weights = jnp.sum(hidden.astype(F32) * back, axis=2)
    return (grad_hidden, grad_weights, grad_down[None])


def solution(mesh):
    dp, expert = mesh.shape["dp"], mesh.shape["expert"]
    shape = (dp // CORES, CORES, expert // (XS * PAIR), PAIR, XS)
    fine = Mesh(mesh.devices.reshape(shape), ("y", "core", "far", "near", "x"))
    tokens = ("y", "core", "far", "near", "x")
    owner = ("far", "near", "x")
    placed = (
        P(tokens, None),
        P(tokens, None, None),
        P(tokens, None),
        P(tokens, None),
        P(owner, None, None),
    )
    return jax.shard_map(
        local,
        mesh=fine,
        in_specs=placed,
        out_specs=(
            P(tokens, None, None),
            P(tokens, None),
            P(owner, ("y", "core"), None),
        ),
        check_vma=False,
    )
```

```python
import functools

import jax
import jax.numpy as jnp
from jax import lax
from jax.experimental import pallas as pl
from jax.experimental.pallas import tpu as pltpu
from jax.sharding import Mesh
from jax.sharding import PartitionSpec as P

CORES = 2
XS = 4
PAIR = 2
DIRECT = 128
PACK_LIMIT = 56 << 20
LANES = 128
F32 = jnp.float32
BF16 = jnp.bfloat16
ROWS = (((0,), (0,)), ((), ()))


def dot(a, b, dims=(((1,), (0,)), ((), ()))):
    return lax.dot_general(a, b, dims, preferred_element_type=F32)


def exchange(value, axes):
    return lax.all_to_all(value, axes, split_axis=0, concat_axis=0, tiled=True)


def over(number, by):
    return (number * (512 // by + 1)) >> 9


def iota(shape, dim):
    return lax.broadcasted_iota(jnp.int32, shape, dim)


def pack_kernel(owners, cap, plane, pieces, *refs):
    sources, (send_ref, pack_ref), inside = refs[:4], refs[4:6], refs[6:10]
    tall_ref, sems = refs[10:]
    copies = [
        pltpu.make_async_copy(source, target, sems.at[i])
        for i, (source, target) in enumerate(zip(sources, inside))
    ]
    for copy in copies:
        copy.start()
    for copy in copies:
        copy.wait()
    ids_ref, combine_ref, hidden_ref, grad_ref = inside
    topk, tok = ids_ref.shape
    pairs, ffw = hidden_ref.shape
    slots = owners * cap
    ids = ids_ref[...]
    owner = (ids & (plane - 1)) * (owners // plane) + (ids >> (plane.bit_length() - 1))
    wide = iota((LANES, tok), 0)
    names = sum((wide == owner[k : k + 1, :]).astype(F32) for k in range(topk))
    earlier = (iota((tok, tok), 0) < iota((tok, tok), 1)).astype(BF16)
    nth = dot(names.astype(BF16), earlier)
    row = iota((slots, LANES), 0)
    row_owner = over(row, cap)
    spread = (row_owner == iota((slots, LANES), 1)).astype(BF16)
    row_names = dot(spread, names.astype(BF16))
    row_nth = dot(spread, nth.astype(BF16))
    row_slot = (row - cap * row_owner).astype(F32)[:, :tok]
    by_token = ((row_names > 0) & (row_nth == row_slot)).astype(BF16)
    lane = iota((tok, pairs), 1)
    first = topk * iota((tok, pairs), 0)
    widen = ((lane >= first) & (lane < first + topk)).astype(BF16)
    own_k = (iota((topk, pairs), 1) & (topk - 1)) == iota((topk, pairs), 0)
    pair_owner = dot(owner.astype(F32).astype(BF16), widen)
    pair_owner = jnp.sum(jnp.where(own_k, pair_owner, 0.0), axis=0, keepdims=True)
    pair_combine = lax.dot_general(
        combine_ref[...],
        widen.astype(F32),
        (((1,), (0,)), ((), ())),
        precision=lax.Precision.HIGHEST,
        preferred_element_type=F32,
    )
    pair_combine = jnp.sum(jnp.where(own_k, pair_combine, 0.0), axis=0, keepdims=True)
    placing = jnp.where(row_owner.astype(F32) == pair_owner, dot(by_token, widen), 0.0)
    scale = jnp.sum(placing * pair_combine, axis=1, keepdims=True)
    piece = grad_ref.shape[1] // pieces
    acts = dot(placing.astype(BF16), hidden_ref[...]) * scale
    direct = [
        dot(by_token, grad_ref[:, c * piece : c * piece + DIRECT]) for c in range(CORES)
    ]
    blocks = [acts[:, at : at + LANES] for at in range(0, ffw, LANES)] + direct
    for i, block in enumerate(blocks):
        tall_ref[pl.ds(i, slots, stride=len(blocks)), :] = block
    send_ref[...] = tall_ref[...].astype(BF16)
    numbers = (names * (nth + 1.0)).astype(BF16)
    same = (iota((tok, tok), 0) == iota((tok, tok), 1)).astype(BF16)
    pack_ref[:, :LANES] = dot(same, numbers, (((1,), (1,)), ((), ()))).astype(BF16)
    at = LANES
    for c in range(CORES):
        for y in range(pieces // CORES):
            start = (y * CORES + c) * piece
            skip = DIRECT if y == 0 else 0
            pack_ref[:, at : at + piece - skip] = grad_ref[:, start + skip : start + piece]
            at += piece - skip


def pick_kernel(far, plane, cap, far_ref, gathered_ref, out_ref):
    tokens = gathered_ref.shape[0]
    tok = tokens // far
    slots = plane * far * cap
    chosen = (iota((plane, LANES), 1) == far * iota((plane, LANES), 0) + far_ref[0]).astype(BF16)
    numbers = dot(chosen, gathered_ref[:, :LANES], (((1,), (1,)), ((), ())))
    row = iota((slots, tokens), 0)
    group = over(row, cap)
    slot = row - cap * group
    row_far, row_plane = group & (far - 1), group >> (far.bit_length() - 1)
    spread = (row_plane[:, :plane] == iota((slots, plane), 1)).astype(BF16)
    numbers = dot(spread, numbers.astype(BF16))
    column_far = iota((slots, tokens), 1) >> (tok.bit_length() - 1)
    picking = jnp.where(
        (column_far == row_far) & (numbers == (slot + 1).astype(F32)), 1.0, 0.0
    ).astype(BF16)
    step = 3 * LANES
    for at in range(0, out_ref.shape[1], step):
        out_ref[:, at : at + step] = dot(
            picking, gathered_ref[:, LANES + at : LANES + at + step]
        ).astype(BF16)


def local(out_grad, hidden, combine, expert_ids, down_weight):
    tok, width = out_grad.shape
    topk = expert_ids.shape[1]
    ffw = hidden.shape[2]
    xs, ys = lax.axis_size("x"), lax.axis_size("y")
    far, near = lax.axis_size("far"), lax.axis_size("near")
    core, far_here = lax.axis_index("core"), lax.axis_index("far")
    owners = far * near * xs
    plane = near * xs
    cap = min(tok, 3 * tok * topk // (2 * owners))
    rows = tok * topk
    slots_here = owners * cap
    half = width // CORES
    piece = half // ys
    relayed = half - DIRECT
    wide = ffw + CORES * DIRECT
    params = pltpu.CompilerParams(vmem_limit_bytes=32 << 20)

    tall = slots_here * wide // LANES
    send, pack = pl.pallas_call(
        functools.partial(pack_kernel, owners, cap, plane, ys * CORES),
        out_shape=(
            jax.ShapeDtypeStruct((tall, LANES), BF16),
            jax.ShapeDtypeStruct((tok, LANES + CORES * relayed), BF16),
        ),
        in_specs=[pl.BlockSpec(memory_space=pl.ANY)] * 4,
        scratch_shapes=[
            pltpu.VMEM((topk, tok), jnp.int32),
            pltpu.VMEM((topk, tok), F32),
            pltpu.VMEM((rows, ffw), BF16),
            pltpu.VMEM((tok, width), BF16),
            pltpu.VMEM((tall, LANES), F32),
            pltpu.SemaphoreType.DMA((4,)),
        ],
        compiler_params=pltpu.CompilerParams(vmem_limit_bytes=PACK_LIMIT),
        name="pack",
    )(expert_ids.T, combine.T, hidden.reshape(rows, ffw), out_grad)
    got = exchange(
        send.reshape(owners, cap * wide // LANES, LANES), ("near", "x", "far")
    ).reshape(slots_here, wide)
    gathered = lax.all_gather(pack, "far", axis=0, tiled=True)

    gathered, got = lax.optimization_barrier((gathered, got))
    relay_rows = pl.pallas_call(
        functools.partial(pick_kernel, far, plane, cap),
        out_shape=jax.ShapeDtypeStruct((slots_here, CORES * relayed), BF16),
        in_specs=[
            pl.BlockSpec(memory_space=pltpu.SMEM),
            pl.BlockSpec(memory_space=pltpu.VMEM),
        ],
        compiler_params=params,
        name="pick",
    )(far_here.astype(jnp.int32).reshape(1), gathered)
    relay = exchange(
        relay_rows.reshape(plane, far * cap, CORES * relayed), ("near", "x")
    ).reshape(slots_here, CORES * relayed)

    swap = [(0, 1), (1, 0)]
    acts = got[:, :ffw]
    both_acts = jnp.concatenate([acts, lax.ppermute(acts, "core", swap)], axis=0)
    weight = down_weight[0].reshape(ys, CORES, piece, ffw).transpose(1, 0, 2, 3)
    weight = weight.reshape(width, ffw)
    relay, both_acts, weight = lax.optimization_barrier((relay, both_acts, weight))

    halves = [
        jnp.concatenate(
            [
                got[:, ffw + c * DIRECT : ffw + (c + 1) * DIRECT],
                relay[:, c * relayed : (c + 1) * relayed],
            ],
            axis=1,
        )
        for c in range(CORES)
    ]
    mine, theirs = [jnp.where(core == 0, halves[c], halves[1 - c]) for c in range(CORES)]
    both_grads = jnp.concatenate([mine, lax.ppermute(theirs, "core", swap)], axis=0)
    partial_value = dot(both_grads, both_acts, ROWS).astype(BF16)
    grad_down = lax.psum_scatter(partial_value, "y", scatter_dimension=0, tiled=True)

    projected = (dot(halves[0], weight[:half]) + dot(halves[1], weight[half:])).astype(BF16)
    returned = exchange(
        projected.reshape(owners, 2, cap * ffw // 2), ("near", "x", "far")
    ).reshape(slots_here, ffw)
    slots = (expert_ids % plane * far + expert_ids // plane).reshape(rows)
    onehot = (slots[:, None] == jnp.arange(owners, dtype=jnp.int32)[None, :]).astype(jnp.int32)
    before = jnp.cumsum(onehot, axis=0) - onehot
    slots = slots * cap + jnp.sum(onehot * before, axis=1)
    placing = slots[None, :] == jnp.arange(slots_here, dtype=jnp.int32)[:, None]
    back = dot(placing.astype(BF16), returned, ROWS).reshape(tok, topk, ffw)
    grad_hidden = (combine[:, :, None] * back).astype(BF16)
    grad_weights = jnp.sum(hidden.astype(F32) * back, axis=2)
    return (grad_hidden, grad_weights, grad_down[None])


def solution(mesh):
    dp, expert = mesh.shape["dp"], mesh.shape["expert"]
    shape = (dp // CORES, CORES, expert // (XS * PAIR), PAIR, XS)
    fine = Mesh(mesh.devices.reshape(shape), ("y", "core", "far", "near", "x"))
    tokens = ("y", "core", "far", "near", "x")
    owner = ("far", "near", "x")
    placed = (
        P(tokens, None),
        P(tokens, None, None),
        P(tokens, None),
        P(tokens, None),
        P(owner, None, None),
    )
    return jax.shard_map(
        local,
        mesh=fine,
        in_specs=placed,
        out_specs=(
            P(tokens, None, None),
            P(tokens, None),
            P(owner, ("y", "core"), None),
        ),
        check_vma=False,
    )
```

```python
import functools

import jax
import jax.numpy as jnp
from jax import lax
from jax.experimental import pallas as pl
from jax.experimental.pallas import tpu as pltpu
from jax.sharding import Mesh
from jax.sharding import PartitionSpec as P

CORES = 2
XS = 4
PAIR = 2
DIRECT = 128
PACK_LIMIT = 56 << 20
LANES = 128
F32 = jnp.float32
BF16 = jnp.bfloat16
ROWS = (((0,), (0,)), ((), ()))


def dot(a, b, dims=(((1,), (0,)), ((), ()))):
    return lax.dot_general(a, b, dims, preferred_element_type=F32)


def exchange(value, axes):
    return lax.all_to_all(value, axes, split_axis=0, concat_axis=0, tiled=True)


def over(number, by):
    return (number * (512 // by + 1)) >> 9


def iota(shape, dim):
    return lax.broadcasted_iota(jnp.int32, shape, dim)


def pack_kernel(owners, cap, plane, pieces, *refs):
    sources, (send_ref, pack_ref), inside = refs[:4], refs[4:6], refs[6:10]
    tall_ref, sems = refs[10:]
    copies = [
        pltpu.make_async_copy(source, target, sems.at[i])
        for i, (source, target) in enumerate(zip(sources, inside))
    ]
    for copy in copies:
        copy.start()
    for copy in copies:
        copy.wait()
    ids_ref, combine_ref, hidden_ref, grad_ref = inside
    topk, tok = ids_ref.shape
    pairs, ffw = hidden_ref.shape
    slots = owners * cap
    ids = ids_ref[...]
    owner = (ids & (plane - 1)) * (owners // plane) + (ids >> (plane.bit_length() - 1))
    wide = iota((LANES, tok), 0)
    names = sum((wide == owner[k : k + 1, :]).astype(F32) for k in range(topk))
    earlier = (iota((tok, tok), 0) < iota((tok, tok), 1)).astype(BF16)
    nth = dot(names.astype(BF16), earlier)
    row = iota((slots, LANES), 0)
    row_owner = over(row, cap)
    spread = (row_owner == iota((slots, LANES), 1)).astype(BF16)
    row_names = dot(spread, names.astype(BF16))
    row_nth = dot(spread, nth.astype(BF16))
    row_slot = (row - cap * row_owner).astype(F32)[:, :tok]
    by_token = ((row_names > 0) & (row_nth == row_slot)).astype(BF16)
    lane = iota((tok, pairs), 1)
    first = topk * iota((tok, pairs), 0)
    widen = ((lane >= first) & (lane < first + topk)).astype(BF16)
    own_k = (iota((topk, pairs), 1) & (topk - 1)) == iota((topk, pairs), 0)
    pair_owner = dot(owner.astype(F32).astype(BF16), widen)
    pair_owner = jnp.sum(jnp.where(own_k, pair_owner, 0.0), axis=0, keepdims=True)
    pair_combine = lax.dot_general(
        combine_ref[...],
        widen.astype(F32),
        (((1,), (0,)), ((), ())),
        precision=lax.Precision.HIGHEST,
        preferred_element_type=F32,
    )
    pair_combine = jnp.sum(jnp.where(own_k, pair_combine, 0.0), axis=0, keepdims=True)
    placing = jnp.where(row_owner.astype(F32) == pair_owner, dot(by_token, widen), 0.0)
    scale = jnp.sum(placing * pair_combine, axis=1, keepdims=True)
    piece = grad_ref.shape[1] // pieces
    acts = dot(placing.astype(BF16), hidden_ref[...]) * scale
    direct = [
        dot(by_token, grad_ref[:, c * piece : c * piece + DIRECT]) for c in range(CORES)
    ]
    blocks = [acts[:, at : at + LANES] for at in range(0, ffw, LANES)] + direct
    for i, block in enumerate(blocks):
        tall_ref[pl.ds(i, slots, stride=len(blocks)), :] = block
    send_ref[...] = tall_ref[...].astype(BF16)
    numbers = (names * (nth + 1.0)).astype(BF16)
    same = (iota((tok, tok), 0) == iota((tok, tok), 1)).astype(BF16)
    pack_ref[:, :LANES] = dot(same, numbers, (((1,), (1,)), ((), ()))).astype(BF16)
    at = LANES
    for c in range(CORES):
        for y in range(pieces // CORES):
            start = (y * CORES + c) * piece
            skip = DIRECT if y == 0 else 0
            pack_ref[:, at : at + piece - skip] = grad_ref[:, start + skip : start + piece]
            at += piece - skip


def pick_kernel(far, plane, cap, far_ref, gathered_ref, out_ref):
    tokens = gathered_ref.shape[0]
    tok = tokens // far
    slots = plane * far * cap
    chosen = (iota((plane, LANES), 1) == far * iota((plane, LANES), 0) + far_ref[0]).astype(BF16)
    numbers = dot(chosen, gathered_ref[:, :LANES], (((1,), (1,)), ((), ())))
    row = iota((slots, tokens), 0)
    group = over(row, cap)
    slot = row - cap * group
    row_far, row_plane = group & (far - 1), group >> (far.bit_length() - 1)
    spread = (row_plane[:, :plane] == iota((slots, plane), 1)).astype(BF16)
    numbers = dot(spread, numbers.astype(BF16))
    column_far = iota((slots, tokens), 1) >> (tok.bit_length() - 1)
    picking = jnp.where(
        (column_far == row_far) & (numbers == (slot + 1).astype(F32)), 1.0, 0.0
    ).astype(BF16)
    step = 3 * LANES
    for at in range(0, out_ref.shape[1], step):
        out_ref[:, at : at + step] = dot(
            picking, gathered_ref[:, LANES + at : LANES + at + step]
        ).astype(BF16)


def local(out_grad, hidden, combine, expert_ids, down_weight):
    tok, width = out_grad.shape
    topk = expert_ids.shape[1]
    ffw = hidden.shape[2]
    xs, ys = lax.axis_size("x"), lax.axis_size("y")
    far, near = lax.axis_size("far"), lax.axis_size("near")
    core, far_here = lax.axis_index("core"), lax.axis_index("far")
    owners = far * near * xs
    plane = near * xs
    cap = min(tok, 3 * tok * topk // (2 * owners))
    rows = tok * topk
    slots_here = owners * cap
    half = width // CORES
    piece = half // ys
    relayed = half - DIRECT
    wide = ffw + CORES * DIRECT
    params = pltpu.CompilerParams(vmem_limit_bytes=32 << 20)

    tall = slots_here * wide // LANES
    send, pack = pl.pallas_call(
        functools.partial(pack_kernel, owners, cap, plane, ys * CORES),
        out_shape=(
            jax.ShapeDtypeStruct((tall, LANES), BF16),
            jax.ShapeDtypeStruct((tok, LANES + CORES * relayed), BF16),
        ),
        in_specs=[pl.BlockSpec(memory_space=pl.ANY)] * 4,
        scratch_shapes=[
            pltpu.VMEM((topk, tok), jnp.int32),
            pltpu.VMEM((topk, tok), F32),
            pltpu.VMEM((rows, ffw), BF16),
            pltpu.VMEM((tok, width), BF16),
            pltpu.VMEM((tall, LANES), F32),
            pltpu.SemaphoreType.DMA((4,)),
        ],
        compiler_params=pltpu.CompilerParams(vmem_limit_bytes=PACK_LIMIT),
        name="pack",
    )(expert_ids.T, combine.T, hidden.reshape(rows, ffw), out_grad)
    got = exchange(
        send.reshape(owners, cap * wide // LANES, LANES), ("near", "x", "far")
    ).reshape(slots_here, wide)
    gathered = lax.all_gather(pack, "far", axis=0, tiled=True)

    gathered, got = lax.optimization_barrier((gathered, got))
    relay_rows = pl.pallas_call(
        functools.partial(pick_kernel, far, plane, cap),
        out_shape=jax.ShapeDtypeStruct((slots_here, CORES * relayed), BF16),
        in_specs=[
            pl.BlockSpec(memory_space=pltpu.SMEM),
            pl.BlockSpec(memory_space=pltpu.VMEM),
        ],
        compiler_params=params,
        name="pick",
    )(far_here.astype(jnp.int32).reshape(1), gathered)
    relay = exchange(
        relay_rows.reshape(plane, far * cap, CORES * relayed), ("near", "x")
    ).reshape(slots_here, CORES * relayed)

    swap = [(0, 1), (1, 0)]
    acts = got[:, :ffw]
    both_acts = jnp.concatenate([acts, lax.ppermute(acts, "core", swap)], axis=0)
    weight = down_weight[0].reshape(ys, CORES, piece, ffw)
    weights = [
        lax.dynamic_index_in_dim(weight, c, 1, keepdims=False).reshape(half, ffw)
        for c in (core, 1 - core)
    ]
    relay, both_acts, weights = lax.optimization_barrier((relay, both_acts, weights))

    halves = [
        jnp.concatenate(
            [
                got[:, ffw + c * DIRECT : ffw + (c + 1) * DIRECT],
                relay[:, c * relayed : (c + 1) * relayed],
            ],
            axis=1,
        )
        for c in range(CORES)
    ]
    mine, theirs = [jnp.where(core == 0, halves[c], halves[1 - c]) for c in range(CORES)]
    both_grads = jnp.concatenate([mine, lax.ppermute(theirs, "core", swap)], axis=0)
    partial_value = dot(both_grads, both_acts, ROWS).astype(BF16)
    grad_down = lax.psum_scatter(partial_value, "y", scatter_dimension=0, tiled=True)

    projected = (dot(mine, weights[0]) + dot(theirs, weights[1])).astype(BF16)
    returned = exchange(
        projected.reshape(owners, 2, cap * ffw // 2), ("near", "x", "far")
    ).reshape(slots_here, ffw)
    slots = (expert_ids % plane * far + expert_ids // plane).reshape(rows)
    onehot = (slots[:, None] == jnp.arange(owners, dtype=jnp.int32)[None, :]).astype(jnp.int32)
    before = jnp.cumsum(onehot, axis=0) - onehot
    slots = slots * cap + jnp.sum(onehot * before, axis=1)
    placing = slots[None, :] == jnp.arange(slots_here, dtype=jnp.int32)[:, None]
    back = dot(placing.astype(BF16), returned, ROWS).reshape(tok, topk, ffw)
    grad_hidden = (combine[:, :, None] * back).astype(BF16)
    grad_weights = jnp.sum(hidden.astype(F32) * back, axis=2)
    return (grad_hidden, grad_weights, grad_down[None])


def solution(mesh):
    dp, expert = mesh.shape["dp"], mesh.shape["expert"]
    shape = (dp // CORES, CORES, expert // (XS * PAIR), PAIR, XS)
    fine = Mesh(mesh.devices.reshape(shape), ("y", "core", "far", "near", "x"))
    tokens = ("y", "core", "far", "near", "x")
    owner = ("far", "near", "x")
    placed = (
        P(tokens, None),
        P(tokens, None, None),
        P(tokens, None),
        P(tokens, None),
        P(owner, None, None),
    )
    return jax.shard_map(
        local,
        mesh=fine,
        in_specs=placed,
        out_specs=(
            P(tokens, None, None),
            P(tokens, None),
            P(owner, ("y", "core"), None),
        ),
        check_vma=False,
    )
```
